256 devices in a mesh: blk: 16 (over z, core), pair: 2 (over x_hi), head: 8 (over y, x_lo).
Axes of the slice: x: 4 (x_hi: 2, x_lo: 2; x = x_hi * 2 + x_lo), y: 4, z: 8, core: 2. Of those that a mesh axis runs over, the one named last changes fastest.
Arguments:
- prefix_query_rows: bfloat16 [2048, 8, 8, 128], P('blk', 'head', 'pair'), may hold values from -6 to 6
- prefix_key_rows: bfloat16 [2048, 8, 128], P('blk', 'head'), may hold values from -6 to 6
- prefix_value_rows: bfloat16 [2048, 8, 128], P('blk', 'head'), may hold values from -6 to 6
- prefix_output_gradient: bfloat16 [2048, 8, 8, 128], P('blk', 'head', 'pair'), may hold values from -6 to 6
- resp_q: bfloat16 [2, 2048, 8, 8, 128], P('pair', 'blk', 'head'), may hold values from -100 to 100
- resp_k: bfloat16 [2, 2048, 8, 128], P('pair', 'blk', 'head'), may hold values from -4 to 4
- response_value_rows: bfloat16 [2, 2048, 8, 128], P('pair', 'blk', 'head'), may hold values from -6 to 6
- response_output_gradient: bfloat16 [2, 2048, 8, 8, 128], P('pair', 'blk', 'head'), may hold values from -6 to 6
- lengths: int32 [2], replicated, may hold values from 128 to 2048, as said below
- prefix_order: int32 [16], replicated, may hold values from 0 to 15, each once
Outputs:
- dprefix_q: bfloat16 [2048, 8, 8, 128], P(('blk', 'head'), None, 'pair')
- dprefix_k: bfloat16 [2048, 8, 128], P(('blk', 'head'))
- dprefix_v: bfloat16 [2048, 8, 128], P(('blk', 'head'))
- dresp_q: bfloat16 [2, 2048, 8, 8, 128], P('pair', ('blk', 'head'))
- dresp_k: bfloat16 [2, 2048, 8, 128], P('pair', ('blk', 'head'))
- dresp_v: bfloat16 [2, 2048, 8, 128], P('pair', ('blk', 'head'))
The draws below stay inside these ranges and needn't reach their ends.
Inputs may be any that keep to these rules, and one draw needn't show every extreme that they name: `prefix_order`: the stored prefix blocks are the prefix blocks 0 to 15, each once. Each length is a multiple of 128; one of the two lengths equals 2048.
All inputs are finite; a program needn't handle non-finite values.
Results may differ from the reference program's by a relative error of at most 0.0051.
Values may be sent and summed in bfloat16 or wider, within the bound.
A program may use at most 128 MiB of HBM per device.

```python
import jax
import jax.numpy as jnp
from jax import lax

HEAD_DIM = 128
KEY_VALUE_HEADS = 8
QUERY_GROUP = 8
PBLK = 128
PREFIX_LENGTH = 2048
RESPONSE_LENGTH = 2048
NPB = 16


def random_key_table(key):
    base_random = jnp.clip(jax.random.normal(jax.random.fold_in(key, 101), (2, RESPONSE_LENGTH, KEY_VALUE_HEADS, HEAD_DIM), jnp.float32), -4.0, 4.0)
    return base_random


def draw_resp_k(key, part):
    return random_key_table(key).astype(jnp.bfloat16)


def draw_resp_q(key, part):
    return jnp.clip(jax.random.normal(jax.random.fold_in(key, 203), (2, RESPONSE_LENGTH, KEY_VALUE_HEADS, QUERY_GROUP, HEAD_DIM), jnp.float32), -4.0, 4.0).astype(jnp.bfloat16)


def draw_lengths(key, part):
    full_side = jax.random.randint(jax.random.fold_in(key, 301), (), 0, 2)
    other = jax.random.randint(jax.random.fold_in(key, 302), (), 1, RESPONSE_LENGTH // PBLK + 1) * PBLK
    return jnp.where(jnp.arange(2) == full_side, RESPONSE_LENGTH, other).astype(jnp.int32)


def levels(key, dims, shards, least, largest):
    def one(position, blocks):
        steps = jax.random.uniform(jax.random.fold_in(jax.random.fold_in(key, 6), position), (blocks,), jnp.float32, least / len(shards), largest / len(shards))
        return jnp.repeat(jnp.exp(steps), dims[position] // blocks).reshape((-1,) + (1,) * (len(dims) - position - 1))

    gain = one(*shards[0])
    for cut in shards[1:]:
        gain = gain * one(*cut)
    return gain


def gaussian(rng, extent, deviation, reach, split=(), kind=jnp.bfloat16):
    values = jax.random.normal(rng, extent, jnp.float32) * deviation
    if len(split) > 0:
        values = levels(rng, extent, split, -0.22, 0.18) * values
    return jnp.clip(values, min=-reach, max=reach).astype(kind)


def setup_inputs(seed: int = 0) -> dict:
    splits = jax.random.split(jax.random.key(seed), 11)
    return {
        "prefix_query_rows": gaussian(splits[0], (PREFIX_LENGTH, KEY_VALUE_HEADS, QUERY_GROUP, HEAD_DIM), 1.0, 6.0, ((0, 16), (1, 8), (2, 2))),
        "prefix_key_rows": gaussian(splits[1], (PREFIX_LENGTH, KEY_VALUE_HEADS, HEAD_DIM), 1.0, 6.0, ((0, 16), (1, 8))),
        "prefix_value_rows": gaussian(splits[2], (PREFIX_LENGTH, KEY_VALUE_HEADS, HEAD_DIM), 1.0, 6.0, ((0, 16), (1, 8))),
        "prefix_output_gradient": gaussian(splits[3], (PREFIX_LENGTH, KEY_VALUE_HEADS, QUERY_GROUP, HEAD_DIM), 1.0, 6.0, ((0, 16), (1, 8), (2, 2))),
        "resp_q": draw_resp_q(jax.random.fold_in(splits[10], 71), 0),
        "resp_k": draw_resp_k(jax.random.fold_in(splits[10], 71), 0),
        "response_value_rows": gaussian(splits[6], (2, RESPONSE_LENGTH, KEY_VALUE_HEADS, HEAD_DIM), 1.0, 6.0, ((0, 2), (1, 16), (2, 8))),
        "response_output_gradient": gaussian(splits[7], (2, RESPONSE_LENGTH, KEY_VALUE_HEADS, QUERY_GROUP, HEAD_DIM), 1.0, 6.0, ((0, 2), (1, 16), (2, 8))),
        "lengths": draw_lengths(jax.random.fold_in(splits[10], 71), 0),
        "prefix_order": jax.random.permutation(splits[9], NPB).astype(jnp.int32),
    }


very_low = -1e30


def attention_grads(queries, query_pos, grad_outs, random_keys, key_pos, values):
    scaling = HEAD_DIM ** -0.5
    logits = jnp.dot(queries, random_keys.T, preferred_element_type=jnp.float32) * scaling
    visible = key_pos[None, :] <= query_pos[:, None]
    peak = jnp.max(jnp.where(visible, logits, very_low), axis=1)
    expo = jnp.where(visible, jnp.exp(logits - peak[:, None]), 0.0)
    log_total = peak + jnp.log(jnp.sum(expo, axis=1))
    softmax = jnp.where(visible, jnp.exp(logits - log_total[:, None]), 0.0)
    dprobs = jnp.dot(grad_outs, values.T, preferred_element_type=jnp.float32)
    deltas = jnp.sum(softmax * dprobs, axis=1)
    dscores = (softmax * (dprobs - deltas[:, None]) * scaling).astype(jnp.bfloat16)
    soft_bf = softmax.astype(jnp.bfloat16)
    grad_q = jnp.dot(dscores, random_keys, preferred_element_type=jnp.float32)
    grad_k = jnp.dot(dscores.T, queries, preferred_element_type=jnp.float32)
    grad_v = jnp.dot(soft_bf.T, grad_outs, preferred_element_type=jnp.float32)
    return grad_q, grad_k, grad_v


def reference(prefix_query_rows, prefix_key_rows, prefix_value_rows, prefix_output_gradient, resp_q, resp_k, response_value_rows, response_output_gradient, lengths, prefix_order):
    prefix_pos = (prefix_order[:, None] * PBLK + jnp.arange(PBLK, dtype=jnp.int32)[None, :]).reshape(PREFIX_LENGTH).astype(jnp.int32)
    resp_pos = (PREFIX_LENGTH + jnp.arange(RESPONSE_LENGTH, dtype=jnp.int32)).astype(jnp.int32)
    key_pos = jnp.concatenate([prefix_pos, resp_pos]).astype(jnp.int32)
    live_rows = jnp.arange(RESPONSE_LENGTH, dtype=jnp.int32)[None, :] < lengths[:, None]
    live_dout = jnp.where(live_rows[:, :, None, None, None], response_output_gradient, jnp.zeros((), response_output_gradient.dtype))

    def per_head(items):
        head_q, head_k, head_v, head_do, rq, rk, rv, rdo = items
        grad_q, grad_k, grad_v = attention_grads(head_q.reshape(PREFIX_LENGTH * QUERY_GROUP, HEAD_DIM), jnp.repeat(prefix_pos, QUERY_GROUP), head_do.reshape(PREFIX_LENGTH * QUERY_GROUP, HEAD_DIM), head_k, prefix_pos, head_v)
        resp_dq = []
        resp_dk = []
        resp_dv = []
        for which_side in range(2):
            random_keys = jnp.concatenate([head_k, rk[which_side]], axis=0)
            values = jnp.concatenate([head_v, rv[which_side]], axis=0)
            part_q, part_k, part_v = attention_grads(rq[which_side].reshape(RESPONSE_LENGTH * QUERY_GROUP, HEAD_DIM), jnp.repeat(resp_pos, QUERY_GROUP), rdo[which_side].reshape(RESPONSE_LENGTH * QUERY_GROUP, HEAD_DIM), random_keys, key_pos, values)
            grad_k = grad_k + part_k[:PREFIX_LENGTH]
            grad_v = grad_v + part_v[:PREFIX_LENGTH]
            resp_dq.append(part_q.reshape(RESPONSE_LENGTH, QUERY_GROUP, HEAD_DIM).astype(jnp.bfloat16))
            resp_dk.append(part_k[PREFIX_LENGTH:].astype(jnp.bfloat16))
            resp_dv.append(part_v[PREFIX_LENGTH:].astype(jnp.bfloat16))
        return (grad_q.reshape(PREFIX_LENGTH, QUERY_GROUP, HEAD_DIM).astype(jnp.bfloat16), grad_k.astype(jnp.bfloat16), grad_v.astype(jnp.bfloat16), jnp.stack(resp_dq), jnp.stack(resp_dk), jnp.stack(resp_dv))

    items = (jnp.moveaxis(prefix_query_rows, 1, 0), jnp.moveaxis(prefix_key_rows, 1, 0), jnp.moveaxis(prefix_value_rows, 1, 0), jnp.moveaxis(prefix_output_gradient, 1, 0), jnp.moveaxis(resp_q, 2, 0), jnp.moveaxis(resp_k, 2, 0), jnp.moveaxis(response_value_rows, 2, 0), jnp.moveaxis(live_dout, 2, 0))
    grad_pq, grad_pk, grad_pv, grad_rq, grad_rk, grad_rv = lax.map(per_head, items)
    return (jnp.moveaxis(grad_pq, 0, 1), jnp.moveaxis(grad_pk, 0, 1), jnp.moveaxis(grad_pv, 0, 1), jnp.moveaxis(grad_rq, 0, 2), jnp.moveaxis(grad_rk, 0, 2), jnp.moveaxis(grad_rv, 0, 2))
```

```python
import functools

import jax
import jax.numpy as jnp
from jax import lax
from jax.experimental import pallas as pl
from jax.experimental.pallas import tpu as pltpu
from jax.sharding import PartitionSpec as P

MESH = pl.DeviceIdType.MESH
F32 = jnp.float32
BF = jnp.bfloat16
I32 = jnp.int32
LANES = 128
SCALE = LANES ** -0.5
C = SCALE * 1.4426950408889634
LOW = -1e30
TW = 512
GW = 256
NP = 512
NR = 1024
NQ = NP + NR


def dot(a, b):
    return lax.dot_general(a, b, (((1,), (0,)), ((), ())), preferred_element_type=F32)


def masked(s, diff, t0, t1, fill):
    n = s.shape[0] // 2
    return jnp.concatenate(
        [jnp.where(diff <= t0, s[:n], fill), jnp.where(diff <= t1, s[n:], fill)], axis=0
    )


def kernel(
    order, lengths, pq, pdo, rq, rdo, pk, pv, rk, rv,
    o_dqp, o_dqr, o_pkv, o_rkv,
    kv, q, do, q_t, do_t, m, l, d, lse, dl, dq_t, diff_p, diff_r,
    s_pre, dp_pre, s_res, dp_res,
    acc, sib_out, sib_in, ring_out, l_in, r_in, fin, dq,
    in_sem, ag_recv, ag_ring_send, ag_sib_send,
    rs_sib_send, rs_sib_recv, rs_send, l_recv, r_recv,
    dq_send, dq_recv, kv_send, kv_recv, px_send, px_recv, loc_sem,
):
    b = lax.axis_index("blk")
    pair = lax.axis_index("pair")
    head = lax.axis_index("head")
    z = b // 2
    c = b % 2
    sib = b + 1 - 2 * c
    right = lax.rem(b + 2, 16)
    left = lax.rem(b + 14, 16)

    barrier = pltpu.get_barrier_semaphore()
    for n in (sib, right, left):
        pl.semaphore_signal(barrier, inc=1, device_id={"blk": n}, device_id_type=MESH)
    for k in range(1, 8):
        pl.semaphore_signal(
            barrier, inc=1, device_id={"head": lax.rem(head + k, 8)}, device_id_type=MESH
        )
    for k in range(8):
        pl.semaphore_signal(
            barrier, inc=1, device_id={"pair": 1 - pair, "head": lax.rem(head + k, 8)},
            device_id_type=MESH,
        )

    def rows_of(block):
        return pl.ds(pl.multiple_of(block * 128, 128), 128)

    loads = [
        pltpu.make_async_copy(ref, kv.at[i, rows_of(b), :], in_sem.at[i])
        for i, ref in enumerate((pk, pv, rk, rv))
    ] + [
        pltpu.make_async_copy(ref, dst, in_sem.at[4 + i])
        for i, (ref, dst) in enumerate((
            (pq, q.at[pl.ds(0, NP), :]),
            (rq, q.at[pl.ds(NP, NR), :]),
            (pdo, do.at[pl.ds(0, NP), :]),
            (rdo, do.at[pl.ds(NP, NR), :]),
        ))
    ]
    for copy in loads:
        copy.start()

    def kv_copy(h, block, send_sem, target):
        piece = kv.at[pl.ds(2 * h, 2), rows_of(block), :]
        return pltpu.make_async_remote_copy(
            src_ref=piece, dst_ref=piece, send_sem=send_sem, recv_sem=ag_recv.at[h, block],
            device_id={"blk": target}, device_id_type=MESH,
        )

    for copy in loads[:4]:
        copy.wait()
    pl.semaphore_wait(barrier, 18)
    for h in range(2):
        kv_copy(h, b, ag_ring_send.at[h, 0], right).start()
        kv_copy(h, b, ag_ring_send.at[h, 4], left).start()
        kv_copy(h, b, ag_sib_send.at[h, 0], sib).start()

    for copy in loads[4:]:
        copy.wait()
    live = b * 128 < lengths[pair]
    do[NP:, :] = jnp.where(live, do[NP:, :].astype(F32), 0.0).astype(BF)
    q_t[...] = q[...].T
    do_t[...] = do[...].T
    m[...] = jnp.full(m.shape, LOW, F32)
    l[...] = jnp.zeros(l.shape, F32)
    d[...] = jnp.zeros(d.shape, F32)
    dq_t[...] = jnp.zeros(dq_t.shape, F32)
    key_row = lax.broadcasted_iota(I32, (128, TW), 0)
    column = lax.broadcasted_iota(I32, (128, TW), 1)
    diff_p[...] = key_row - column // 4
    diff_r[...] = key_row - column // 8

    def thresholds(zp, h, tile):
        if h == 0:
            if tile > 0:
                return ()
            own = order[b]
            return (diff_p[...], (own - order[2 * zp]) * 128, (own - order[2 * zp + 1]) * 128)
        t0 = (b - 2 * zp) * 128 + (tile - 1) * (TW // 8)
        return (diff_r[...], t0, t0 - 128)

    def keys_of(zp, h):
        rows = pl.ds(pl.multiple_of(zp * 256, 256), 256)
        return kv[2 * h, rows, :], kv[2 * h + 1, rows, :]

    stored = ((s_pre, dp_pre), (s_res, dp_res))

    def totals_unit(zp, h):
        k, v = keys_of(zp, h)
        rows = pl.ds(pl.multiple_of(zp * 256, 256), 256)
        for tile in range(h, NQ // TW):
            cs = pl.ds(tile * TW, TW)
            s = dot(k, q_t[:, cs]) * C
            dp = dot(v, do_t[:, cs])
            limits = thresholds(zp, h, tile)
            if limits:
                s = masked(s, *limits, LOW)
            there = pl.ds((tile - h) * TW, TW)
            stored[h][0][rows, there] = s
            stored[h][1][rows, there] = dp
            s = s.reshape(-1, 8, TW)
            dp = dp.reshape(-1, 8, TW)
            old = m[:, cs]
            new = jnp.maximum(old, jnp.max(s, axis=0))
            e = jnp.exp2(s - new[None])
            shrink = jnp.exp2(old - new)
            m[:, cs] = new
            l[:, cs] = l[:, cs] * shrink + jnp.sum(e, axis=0)
            d[:, cs] = d[:, cs] * shrink + jnp.sum(e * dp, axis=0)

    def take_ring(t):
        k = (t + 1) // 2
        for h in range(2):
            @pl.when(t % 2 == 1)
            def _():
                block = lax.rem(b + 16 - 2 * k, 16)
                kv_copy(h, block, ag_ring_send.at[h, 0], right).wait_recv()

                @pl.when(k < 4)
                def _():
                    kv_copy(h, block, ag_ring_send.at[h, k], right).start()

                kv_copy(h, block, ag_sib_send.at[h, t], sib).start()

            @pl.when(t % 2 == 0)
            def _():
                block = lax.rem(b + 2 * k, 16)
                kv_copy(h, block, ag_ring_send.at[h, 0], left).wait_recv()

                @pl.when(k < 3)
                def _():
                    kv_copy(h, block, ag_ring_send.at[h, 4 + k], left).start()

                kv_copy(h, block, ag_sib_send.at[h, t], sib).start()

    def totals_step(t, carry):
        @pl.when(t < 7)
        def _():
            take_ring(t + 1)

        k = (t + 1) // 2
        zp = lax.rem(jnp.where(t % 2 == 1, z + 8 - k, z + k), 8)
        for h in range(2):
            kv_copy(h, 2 * zp + 1 - c, ag_sib_send.at[h, 0], sib).wait_recv()
        totals_unit(zp, 0)

        @pl.when(zp <= z)
        def _():
            totals_unit(zp, 1)

        return carry

    lax.fori_loop(0, 8, totals_step, 0)

    top = jnp.max(m[...], axis=0, keepdims=True)
    weight = jnp.exp2(m[...] - top)
    total = jnp.sum(l[...] * weight, axis=0, keepdims=True)
    lse[...] = top + jnp.log2(total)
    dl[...] = jnp.sum(d[...] * weight, axis=0, keepdims=True) / total

    def grads_unit(zp, h):
        rows = pl.ds(pl.multiple_of(zp * 256, 256), 256)
        k_t = kv[2 * h, rows, :].T
        dk = jnp.zeros((256, LANES), F32)
        dv = jnp.zeros((256, LANES), F32)
        for tile in range((NQ - h * NP) // GW):
            there = pl.ds(tile * GW, GW)
            cs = pl.ds(h * NP + tile * GW, GW)
            p = jnp.exp2(stored[h][0][rows, there] - lse[:, cs])
            ds = (p * (stored[h][1][rows, there] - dl[:, cs]) * SCALE).astype(BF)
            dk += dot(ds, q[cs, :])
            dv += dot(p.astype(BF), do[cs, :])
            dq_t[:, cs] += dot(k_t, ds)
        for i, part in ((0, dk), (1, dv)):
            acc[h, 0, i] = part[:128]
            acc[h, 1, i] = part[128:]

    def sib_copy(t, h):
        return pltpu.make_async_remote_copy(
            src_ref=sib_out.at[t, h], dst_ref=sib_in.at[t, h], send_sem=rs_sib_send.at[t, h],
            recv_sem=rs_sib_recv.at[t, h], device_id={"blk": sib}, device_id_type=MESH,
        )

    def left_copy(dist, h):
        return pltpu.make_async_remote_copy(
            src_ref=ring_out.at[dist - 1, h], dst_ref=l_in.at[dist - 1, h],
            send_sem=rs_send.at[dist - 1, h], recv_sem=l_recv.at[dist - 1, h],
            device_id={"blk": left}, device_id_type=MESH,
        )

    def right_copy(dist, h):
        return pltpu.make_async_remote_copy(
            src_ref=ring_out.at[dist + 3, h], dst_ref=r_in.at[dist - 1, h],
            send_sem=rs_send.at[dist + 3, h], recv_sem=r_recv.at[dist - 1, h],
            device_id={"blk": right}, device_id_type=MESH,
        )

    def compute(t, h):
        half = (t + 1) // 2
        zp = lax.rem(jnp.where(t % 2 == 0, z + 4 + half, z + 12 - half), 8)
        if h == 0:
            grads_unit(zp, 0)
        else:
            @pl.when(zp <= z)
            def _():
                grads_unit(zp, 1)

            @pl.when(zp > z)
            def _():
                acc[1] = jnp.zeros(acc.shape[1:], F32)

        sib_out[t, h] = acc[h, 1 - c].astype(BF)
        sib_copy(t, h).start()

    def own_and_sibling(t, h):
        sib_copy(t, h).wait_recv()
        return acc[h, c] + sib_in[t, h].astype(F32)

    def finalize(t, h):
        half = (t + 1) // 2
        dist = 4 - half
        part = own_and_sibling(t, h)

        @pl.when(t % 2 == 0)
        def _():
            @pl.when(dist == 4)
            def _():
                ring_out[dist - 1, h] = part.astype(BF)

            @pl.when(dist < 4)
            def _():
                left_copy(dist + 1, h).wait_recv()
                ring_out[dist - 1, h] = (part + l_in[dist, h].astype(F32)).astype(BF)

            left_copy(dist, h).start()

        @pl.when(t % 2 == 1)
        def _():
            @pl.when(dist == 3)
            def _():
                ring_out[dist + 3, h] = part.astype(BF)

            @pl.when(dist < 3)
            def _():
                right_copy(dist + 1, h).wait_recv()
                ring_out[dist + 3, h] = (part + r_in[dist, h].astype(F32)).astype(BF)

            right_copy(dist, h).start()

    def grads_step(t, carry):
        compute(t, 0)

        @pl.when(t > 0)
        def _():
            finalize(t - 1, 1)

        compute(t, 1)

        @pl.when(t < 7)
        def _():
            finalize(t, 0)

        return carry

    lax.fori_loop(0, 8, grads_step, 0)

    def peer(k, other):
        where = {"head": lax.rem(head + k, 8)}
        if other:
            where["pair"] = 1 - pair
        return where

    def to_heads(k, src, dst, send_sem, recv_sem, other=False):
        return pltpu.make_async_remote_copy(
            src_ref=src, dst_ref=dst, send_sem=send_sem, recv_sem=recv_sem,
            device_id=peer(k, other), device_id_type=MESH,
        )

    def dq_copies(k):
        h = lax.rem(head + k, 8)
        rows_p = dq.at[pl.ds(pl.multiple_of(h * 64, 64), 64), :]
        rows_r = dq.at[pl.ds(pl.multiple_of(NP + h * 128, 128), 128), :]
        return ((rows_p, o_dqp.at[head]), (rows_r, o_dqr.at[head]))

    def kv_pieces(k):
        h = lax.rem(head + k, 8)
        rows = pl.ds(pl.multiple_of(h * 16, 16), 16)
        return (fin.at[0, :, rows, :], o_pkv.at[pair, :, head]), (
            fin.at[1, :, rows, :], o_rkv.at[:, head])

    dq[...] = dq_t[...].T.astype(BF)
    pending = []
    local = []
    for k in range(1, 8):
        for i, (src, dst) in enumerate(dq_copies(k)):
            copy = to_heads(k, src, dst, dq_send.at[i, k], dq_recv.at[i, k])
            copy.start()
            pending.append(copy)
    for i, (src, dst) in enumerate(dq_copies(0)):
        copy = pltpu.make_async_copy(src, dst, loc_sem.at[i])
        copy.start()
        local.append(copy)

    for h in range(2):
        part = own_and_sibling(7, h)
        left_copy(1, h).wait_recv()
        right_copy(1, h).wait_recv()
        fin[h] = (part + l_in[0, h].astype(F32) + r_in[0, h].astype(F32)).astype(BF)
    for k in range(0, 8):
        src, dst = kv_pieces(k)[0]
        copy = to_heads(k, src, dst, px_send.at[k], px_recv.at[k], other=True)
        copy.start()
        pending.append(copy)
    for k in range(1, 8):
        for i, (src, dst) in enumerate(kv_pieces(k)):
            copy = to_heads(k, src, dst, kv_send.at[i, k], kv_recv.at[i, k])
            copy.start()
            pending.append(copy)
    for i, (src, dst) in enumerate(kv_pieces(0)):
        copy = pltpu.make_async_copy(src, dst, loc_sem.at[2 + i])
        copy.start()
        local.append(copy)

    for h in range(2):
        for k in range(7):
            kv_copy(h, b, ag_ring_send.at[h, k], right).wait_send()
        for k in range(8):
            kv_copy(h, b, ag_sib_send.at[h, k], sib).wait_send()
        for t in range(8):
            sib_copy(t, h).wait_send()
        for dist in range(1, 5):
            left_copy(dist, h).wait_send()
        for dist in range(1, 4):
            right_copy(dist, h).wait_send()
    for copy in local:
        copy.wait()
    for copy in pending:
        copy.wait()


def place(dqp, dqr, pkv, rkv, o_pq, o_pk, o_pv, o_rq, o_rk, o_rv, b_pq, b_rq, b_kv, sems):
    copies = []

    def send(i, src, dst):
        copy = pltpu.make_async_copy(src, dst, sems.at[i])
        copy.start()
        copies.append(copy)

    for g in range(8):
        b_rq[:, g] = dqr[g]
    send(0, b_rq, o_rq)
    for g in range(8):
        b_pq[:, g] = dqp[g]
    send(1, b_pq, o_pq)
    to = lax.broadcasted_iota(I32, (128, 128), 0)
    source = lax.broadcasted_iota(I32, (128, 128), 1)
    move = jnp.where(source == (to % 8) * 16 + to // 8, 1.0, 0.0).astype(BF)
    for i, out in enumerate((o_pk, o_pv, o_rk, o_rv)):
        if i < 2:
            rows = dot(move, pkv[0, i]) + dot(move, pkv[1, i])
        else:
            rows = dot(move, rkv[i - 2])
        b_kv[i] = rows.astype(BF)
        send(2 + i, b_kv.at[i], out)
    for copy in copies:
        copy.wait()


def on_device(
    prefix_query_rows,
    prefix_key_rows,
    prefix_value_rows,
    prefix_output_gradient,
    resp_q,
    resp_k,
    response_value_rows,
    response_output_gradient,
    lengths,
    prefix_order,
):
    vm = pltpu.VMEM
    dma = pltpu.SemaphoreType.DMA
    out = jax.ShapeDtypeStruct
    dqp, dqr, pkv, rkv = pl.pallas_call(
        kernel,
        out_shape=(
            out((8, 64, LANES), BF),
            out((8, 128, LANES), BF),
            out((2, 2, 8, 16, LANES), BF),
            out((2, 8, 16, LANES), BF),
        ),
        in_specs=[pl.BlockSpec(memory_space=pltpu.SMEM)] * 2
        + [pl.BlockSpec(memory_space=pltpu.HBM)] * 8,
        out_specs=[pl.BlockSpec(memory_space=pl.ANY)] * 4,
        scratch_shapes=[
            vm((4, 2048, LANES), BF),
            vm((NQ, LANES), BF),
            vm((NQ, LANES), BF),
            vm((LANES, NQ), BF),
            vm((LANES, NQ), BF),
            vm((8, NQ), F32),
            vm((8, NQ), F32),
            vm((8, NQ), F32),
            vm((1, NQ), F32),
            vm((1, NQ), F32),
            vm((LANES, NQ), F32),
            vm((128, TW), I32),
            vm((128, TW), I32),
            vm((2048, NQ), F32),
            vm((2048, NQ), F32),
            vm((2048, NR), F32),
            vm((2048, NR), F32),
            vm((2, 2, 2, 128, LANES), F32),
            vm((8, 2, 2, 128, LANES), BF),
            vm((8, 2, 2, 128, LANES), BF),
            vm((7, 2, 2, 128, LANES), BF),
            vm((4, 2, 2, 128, LANES), BF),
            vm((3, 2, 2, 128, LANES), BF),
            vm((2, 2, 128, LANES), BF),
            vm((NQ, LANES), BF),
            dma((8,)),
            dma((2, 16)),
            dma((2, 7)),
            dma((2, 8)),
            dma((8, 2)),
            dma((8, 2)),
            dma((7, 2)),
            dma((4, 2)),
            dma((3, 2)),
            dma((2, 8)),
            dma((2, 8)),
            dma((2, 8)),
            dma((2, 8)),
            dma((8,)),
            dma((8,)),
            dma((4,)),
        ],
        compiler_params=pltpu.CompilerParams(
            collective_id=0, has_side_effects=True, vmem_limit_bytes=56 << 20
        ),
    )(
        prefix_order,
        lengths,
        prefix_query_rows.reshape(NP, LANES),
        prefix_output_gradient.reshape(NP, LANES),
        resp_q.reshape(NR, LANES),
        response_output_gradient.reshape(NR, LANES),
        prefix_key_rows.reshape(128, LANES),
        prefix_value_rows.reshape(128, LANES),
        resp_k.reshape(128, LANES),
        response_value_rows.reshape(128, LANES),
    )
    any_space = pl.BlockSpec(memory_space=pl.ANY)
    vmem_space = pl.BlockSpec(memory_space=pltpu.VMEM)
    return pl.pallas_call(
        place,
        out_shape=(
            out((16, 8, 4, LANES), BF),
            out((128, LANES), BF),
            out((128, LANES), BF),
            out((16, 8, 8, LANES), BF),
            out((128, LANES), BF),
            out((128, LANES), BF),
        ),
        in_specs=[vmem_space] * 4,
        out_specs=[any_space] * 6,
        scratch_shapes=[
            vm((16, 8, 4, LANES), BF),
            vm((16, 8, 8, LANES), BF),
            vm((4, 128, LANES), BF),
            dma((6,)),
        ],
    )(
        dqp.reshape(8, 16, 4, LANES),
        dqr.reshape(8, 16, 8, LANES),
        pkv.reshape(2, 2, 128, LANES),
        rkv.reshape(2, 128, LANES),
    )


def shaped(*args):
    pq, pk, pv, rq, rk, rv = on_device(*args)
    keys = (16, 8, LANES)
    return (
        pq, pk.reshape(keys), pv.reshape(keys),
        rq[None], rk.reshape(keys)[None], rv.reshape(keys)[None],
    )


def solution(mesh):
    in_specs = (
        P("blk", "head", "pair", None),
        P("blk", "head", None),
        P("blk", "head", None),
        P("blk", "head", "pair", None),
        P("pair", "blk", "head", None, None),
        P("pair", "blk", "head", None),
        P("pair", "blk", "head", None),
        P("pair", "blk", "head", None, None),
        P(),
        P(),
    )
    out_specs = (
        P(("blk", "head"), None, "pair", None),
        P(("blk", "head"), None, None),
        P(("blk", "head"), None, None),
        P("pair", ("blk", "head"), None, None, None),
        P("pair", ("blk", "head"), None, None),
        P("pair", ("blk", "head"), None, None),
    )
    return jax.shard_map(
        shaped, mesh=mesh, in_specs=in_specs, out_specs=out_specs, check_vma=False
    )
```

```python
import functools

import jax
import jax.numpy as jnp
from jax import lax
from jax.experimental import pallas as pl
from jax.experimental.pallas import tpu as pltpu
from jax.sharding import PartitionSpec as P

MESH = pl.DeviceIdType.MESH
F32 = jnp.float32
BF = jnp.bfloat16
I32 = jnp.int32
LANES = 128
SCALE = LANES ** -0.5
C = SCALE * 1.4426950408889634
LOW = -1e30
TW = 512
GW = 256
NP = 512
NR = 1024
NQ = NP + NR


def dot(a, b):
    return lax.dot_general(a, b, (((1,), (0,)), ((), ())), preferred_element_type=F32)


def masked(s, diff, t0, t1, fill):
    n = s.shape[0] // 2
    return jnp.concatenate(
        [jnp.where(diff <= t0, s[:n], fill), jnp.where(diff <= t1, s[n:], fill)], axis=0
    )


def kernel(
    order_in, lengths_in, pq, pdo, rq, rdo, pk, pv, rk, rv,
    o_dqp, o_dqr, o_own, o_other,
    order, lengths,
    kv, q, do, q_t, do_t, m, l, d, lse, dl, dq_t, diff_p, diff_r,
    s_pre, dp_pre, s_res, dp_res,
    acc, sib_out, sib_in, ring_out, l_in, r_in, far_in, fin, dq,
    in_sem, ag_recv, ag_ring_send, ag_sib_send,
    rs_sib_send, rs_sib_recv, rs_send, l_recv, r_recv, far_recv,
    end_send, end_recv, loc_sem,
):
    b = lax.axis_index("blk")
    pair = lax.axis_index("pair")
    head = lax.axis_index("head")
    z = b // 2
    c = b % 2
    sib = b + 1 - 2 * c
    right = lax.rem(b + 2, 16)
    left = lax.rem(b + 14, 16)
    right2 = lax.rem(b + 4, 16)
    left2 = lax.rem(b + 12, 16)

    def rows_of(block):
        return pl.ds(pl.multiple_of(block * 128, 128), 128)

    loads = [
        pltpu.make_async_copy(ref, kv.at[i, rows_of(b), :], in_sem.at[i])
        for i, ref in enumerate((pk, pv, rk, rv))
    ] + [
        pltpu.make_async_copy(ref, dst, in_sem.at[4 + i])
        for i, (ref, dst) in enumerate((
            (pq, q.at[pl.ds(0, NP), :]),
            (rq, q.at[pl.ds(NP, NR), :]),
            (pdo, do.at[pl.ds(0, NP), :]),
            (rdo, do.at[pl.ds(NP, NR), :]),
            (order_in, order),
            (lengths_in, lengths),
        ))
    ]
    barrier = pltpu.get_barrier_semaphore()
    for n in (sib, right, left, right2, left2):
        pl.semaphore_signal(barrier, inc=1, device_id={"blk": n}, device_id_type=MESH)
    for k in range(1, 8):
        pl.semaphore_signal(
            barrier, inc=1, device_id={"head": lax.rem(head + k, 8)}, device_id_type=MESH
        )
    for k in range(8):
        pl.semaphore_signal(
            barrier, inc=1, device_id={"pair": 1 - pair, "head": lax.rem(head + k, 8)},
            device_id_type=MESH,
        )

    for copy in loads:
        copy.start()

    def kv_copy(i, block, send_sem, target):
        piece = kv.at[i, rows_of(block), :]
        return pltpu.make_async_remote_copy(
            src_ref=piece, dst_ref=piece, send_sem=send_sem, recv_sem=ag_recv.at[i, block],
            device_id={"blk": target}, device_id_type=MESH,
        )

    for copy in loads[:4]:
        copy.wait()
    pl.semaphore_wait(barrier, 20)
    for i in range(4):
        kv_copy(i, b, ag_ring_send, right).start()
        kv_copy(i, b, ag_ring_send, left).start()
        kv_copy(i, b, ag_sib_send, sib).start()

    for copy in loads[4:]:
        copy.wait()
    live = b * 128 < lengths[pair]
    do[NP:, :] = jnp.where(live, do[NP:, :].astype(F32), 0.0).astype(BF)
    q_t[...] = q[...].T
    do_t[...] = do[...].T
    m[...] = jnp.full(m.shape, LOW, F32)
    l[...] = jnp.zeros(l.shape, F32)
    d[...] = jnp.zeros(d.shape, F32)
    dq_t[...] = jnp.zeros(dq_t.shape, F32)
    key_row = lax.broadcasted_iota(I32, (128, TW), 0)
    column = lax.broadcasted_iota(I32, (128, TW), 1)
    diff_p[...] = key_row - column // 4
    diff_r[...] = key_row - column // 8

    def thresholds(zp, h, tile):
        if h == 0:
            if tile > 0:
                return ()
            own = order[b]
            return (diff_p[...], (own - order[2 * zp]) * 128, (own - order[2 * zp + 1]) * 128)
        t0 = (b - 2 * zp) * 128 + (tile - 1) * (TW // 8)
        return (diff_r[...], t0, t0 - 128)

    def keys_of(zp, h):
        rows = pl.ds(pl.multiple_of(zp * 256, 256), 256)
        return kv[2 * h, rows, :], kv[2 * h + 1, rows, :]

    stored = ((s_pre, dp_pre), (s_res, dp_res))

    def totals_unit(zp, h):
        k, v = keys_of(zp, h)
        rows = pl.ds(pl.multiple_of(zp * 256, 256), 256)
        for tile in range(h, NQ // TW):
            cs = pl.ds(tile * TW, TW)
            s = dot(k, q_t[:, cs]) * C
            dp = dot(v, do_t[:, cs])
            limits = thresholds(zp, h, tile)
            if limits:
                s = masked(s, *limits, LOW)
            there = pl.ds((tile - h) * TW, TW)
            stored[h][0][rows, there] = s
            stored[h][1][rows, there] = dp
            s = s.reshape(-1, 8, TW)
            dp = dp.reshape(-1, 8, TW)
            old = m[:, cs]
            new = jnp.maximum(old, jnp.max(s, axis=0))
            e = jnp.exp2(s - new[None])
            shrink = jnp.exp2(old - new)
            m[:, cs] = new
            l[:, cs] = l[:, cs] * shrink + jnp.sum(e, axis=0)
            d[:, cs] = d[:, cs] * shrink + jnp.sum(e * dp, axis=0)

    def take_ring(k):
        from_left = lax.rem(b + 16 - 2 * k, 16)
        from_right = lax.rem(b + 2 * k, 16)

        def take(i, block, target, go_on):
            kv_copy(i, block, ag_ring_send, target).wait_recv()

            @pl.when(go_on)
            def _():
                kv_copy(i, block, ag_ring_send, target).start()

            kv_copy(i, block, ag_sib_send, sib).start()

        for i in range(4):
            there = i < 2

            @pl.when((k < 4) | there)
            def _():
                take(i, from_left, right, (k < 3) | ((k == 3) & there))

            @pl.when((k < 4) | (not there))
            def _():
                take(i, from_right, left, (k < 3) | ((k == 3) & (not there)))

    def totals_step(n, carry):
        @pl.when((n == 0) | (n == 1) | (n == 3) | (n == 7))
        def _():
            take_ring(jnp.where(n == 0, 1, jnp.where(n == 7, 4, (n + 3) // 2)))

        k = (n + 1) // 2
        zp = lax.rem(jnp.where(n % 2 == 1, z + 8 - k, z + k), 8)
        for i in range(4):
            kv_copy(i, 2 * zp + 1 - c, ag_sib_send, sib).wait_recv()
        totals_unit(zp, 0)

        @pl.when(zp <= z)
        def _():
            totals_unit(zp, 1)

        return carry

    lax.fori_loop(0, 8, totals_step, 0)

    top = jnp.max(m[...], axis=0, keepdims=True)
    weight = jnp.exp2(m[...] - top)
    total = jnp.sum(l[...] * weight, axis=0, keepdims=True)
    lse[...] = top + jnp.log2(total)
    dl[...] = jnp.sum(d[...] * weight, axis=0, keepdims=True) / total

    def grads_unit(zp, h, slot):
        rows = pl.ds(pl.multiple_of(zp * 256, 256), 256)
        k_t = kv[2 * h, rows, :].T
        dk = jnp.zeros((256, LANES), F32)
        dv = jnp.zeros((256, LANES), F32)
        for tile in range((NQ - h * NP) // GW):
            there = pl.ds(tile * GW, GW)
            cs = pl.ds(h * NP + tile * GW, GW)
            p = jnp.exp2(stored[h][0][rows, there] - lse[:, cs])
            ds = (p * (stored[h][1][rows, there] - dl[:, cs]) * SCALE).astype(BF)
            dk += dot(ds, q[cs, :])
            dv += dot(p.astype(BF), do[cs, :])
            dq_t[:, cs] += dot(k_t, ds)
        for i, part in ((0, dk), (1, dv)):
            acc[slot, h, 0, i] = part[:128]
            acc[slot, h, 1, i] = part[128:]

    def sib_copy(t, h):
        return pltpu.make_async_remote_copy(
            src_ref=sib_out.at[t, h], dst_ref=sib_in.at[t, h], send_sem=rs_sib_send,
            recv_sem=rs_sib_recv.at[t, h], device_id={"blk": sib}, device_id_type=MESH,
        )

    def left_copy(k, h, i):
        return pltpu.make_async_remote_copy(
            src_ref=ring_out.at[k - 1, h, i], dst_ref=l_in.at[k - 1, h, i],
            send_sem=rs_send, recv_sem=l_recv.at[k - 1, h, i],
            device_id={"blk": left}, device_id_type=MESH,
        )

    def right_copy(k, h, i):
        return pltpu.make_async_remote_copy(
            src_ref=ring_out.at[k + 2, h, i], dst_ref=r_in.at[k - 1, h, i],
            send_sem=rs_send, recv_sem=r_recv.at[k - 1, h, i],
            device_id={"blk": right}, device_id_type=MESH,
        )

    def far_copy(h, i):
        return pltpu.make_async_remote_copy(
            src_ref=ring_out.at[6, h, i], dst_ref=far_in.at[h, i],
            send_sem=rs_send, recv_sem=far_recv.at[h, i],
            device_id={"blk": (left2, right2)[h]}, device_id_type=MESH,
        )

    def compute(t, h):
        k = jnp.where(t == 0, 4, 3 - (t - 1) // 2)
        zp = lax.rem(jnp.where(t % 2 == 1, z + 8 - k, z + k), 8)
        slot = t % 2
        if h == 0:
            grads_unit(zp, 0, slot)
        else:
            @pl.when(zp <= z)
            def _():
                grads_unit(zp, 1, slot)

            @pl.when(zp > z)
            def _():
                acc[slot, 1] = jnp.zeros(acc.shape[2:], F32)

        sib_out[t, h] = acc[slot, h, 1 - c].astype(BF)
        sib_copy(t, h).start()

    def finalize(t, h):
        k = 3 - (t - 1) // 2
        slot = t % 2
        sib_copy(t, h).wait_recv()
        for i in range(2):
            acc[slot, h, c, i] = acc[slot, h, c, i] + sib_in[t, h, i].astype(F32)

        def pass_on(place_of, copy_of, into, with_far):
            for i in range(2):
                @pl.when(k < 3)
                def _():
                    copy_of(k + 1, h, i).wait_recv()
                    acc[slot, h, c, i] = acc[slot, h, c, i] + into[k, h, i].astype(F32)

                if with_far:
                    @pl.when(k == 2)
                    def _():
                        far_copy(h, i).wait_recv()
                        acc[slot, h, c, i] = acc[slot, h, c, i] + far_in[h, i].astype(F32)

                ring_out[place_of, h, i] = acc[slot, h, c, i].astype(BF)
                copy_of(k, h, i).start()

        @pl.when(t == 0)
        def _():
            for i in range(2):
                ring_out[6, h, i] = acc[slot, h, c, i].astype(BF)
                far_copy(h, i).start()

        @pl.when(t % 2 == 1)
        def _():
            pass_on(k - 1, left_copy, l_in, h == 0)

        @pl.when((t % 2 == 0) & (t > 0))
        def _():
            pass_on(k + 2, right_copy, r_in, h == 1)

    def grads_step(t, carry):
        for h in range(2):
            compute(t, h)

            @pl.when(t > 0)
            def _():
                finalize(t - 1, h)

        return carry

    lax.fori_loop(0, 8, grads_step, 0)

    def peer(k, other):
        where = {"head": lax.rem(head + k, 8)}
        if other:
            where["pair"] = 1 - pair
        return where

    def to_heads(k, src, dst, send_sem, recv_sem, other=False):
        return pltpu.make_async_remote_copy(
            src_ref=src, dst_ref=dst, send_sem=send_sem, recv_sem=recv_sem,
            device_id=peer(k, other), device_id_type=MESH,
        )

    def dq_copies(k):
        h = lax.rem(head + k, 8)
        rows_p = dq.at[pl.ds(pl.multiple_of(h * 64, 64), 64), :]
        rows_r = dq.at[pl.ds(pl.multiple_of(NP + h * 128, 128), 128), :]
        return ((rows_p, o_dqp.at[head]), (rows_r, o_dqr.at[head]))

    def kv_rows(k):
        return pl.ds(pl.multiple_of(lax.rem(head + k, 8) * 16, 16), 16)

    dq[...] = dq_t[...].T.astype(BF)
    local = []
    for k in range(1, 8):
        for i, (src, dst) in enumerate(dq_copies(k)):
            to_heads(k, src, dst, end_send.at[i], end_recv.at[i]).start()
    for i, (src, dst) in enumerate(dq_copies(0)):
        copy = pltpu.make_async_copy(src, dst, loc_sem.at[i])
        copy.start()
        local.append(copy)

    for h in range(2):
        sib_copy(7, h).wait_recv()
        for i in range(2):
            part = acc[1, h, c, i] + sib_in[7, h, i].astype(F32)
            left_copy(1, h, i).wait_recv()
            right_copy(1, h, i).wait_recv()
            part = part + l_in[0, h, i].astype(F32) + r_in[0, h, i].astype(F32)
            fin[h, i] = part.astype(BF)
    for k in range(8):
        to_heads(
            k, fin.at[0, :, kv_rows(k), :], o_other.at[head], end_send.at[3], end_recv.at[3], other=True
        ).start()
    for k in range(1, 8):
        to_heads(
            k, fin.at[:, :, kv_rows(k), :], o_own.at[head], end_send.at[2], end_recv.at[2]
        ).start()
    copy = pltpu.make_async_copy(fin.at[:, :, kv_rows(0), :], o_own.at[head], loc_sem.at[2])
    copy.start()
    local.append(copy)

    def wait_sends(ref, sem):
        pltpu.make_async_copy(ref, ref, sem).wait()

    wait_sends(kv.at[:, pl.ds(0, 7 * 128), :], ag_ring_send)
    wait_sends(kv.at[:, pl.ds(0, 8 * 128), :], ag_sib_send)
    wait_sends(sib_out, rs_sib_send)
    wait_sends(ring_out, rs_send)
    wait_sends(dq.at[pl.ds(0, 7 * 64), :], end_send.at[0])
    wait_sends(dq.at[pl.ds(0, 7 * 128), :], end_send.at[1])
    wait_sends(fin.at[:, :, pl.ds(0, 7 * 16), :], end_send.at[2])
    wait_sends(fin.at[0], end_send.at[3])
    for copy in local:
        copy.wait()
    for sem, ref in enumerate((o_dqp, o_dqr, o_own)):
        wait_sends(ref.at[pl.ds(0, 7)], end_recv.at[sem])
    wait_sends(o_other, end_recv.at[3])


def place(
    i_dqp, i_dqr, i_own, i_other, o_pq, o_pk, o_pv, o_rq, o_rk, o_rv,
    dqp, dqr, own, other, b_pq, b_rq, b_kv, in_sems, sems,
):
    loads = [
        pltpu.make_async_copy(src, dst, in_sems.at[i])
        for i, (src, dst) in enumerate(((i_dqp, dqp), (i_dqr, dqr), (i_own, own), (i_other, other)))
    ]
    for load in loads:
        load.start()
    copies = []

    def send(i, src, dst):
        copy = pltpu.make_async_copy(src, dst, sems.at[i])
        copy.start()
        copies.append(copy)

    loads[1].wait()
    for g in range(8):
        b_rq[:, g] = dqr[g]
    send(0, b_rq, o_rq)
    loads[0].wait()
    for g in range(8):
        b_pq[:, g] = dqp[g]
    send(1, b_pq, o_pq)
    to = lax.broadcasted_iota(I32, (128, 128), 0)
    source = lax.broadcasted_iota(I32, (128, 128), 1)
    move = jnp.where(source == (to % 8) * 16 + to // 8, 1.0, 0.0).astype(BF)
    loads[2].wait()
    loads[3].wait()
    for i, out in enumerate((o_pk, o_pv, o_rk, o_rv)):
        rows = dot(move, own[:, i // 2, i % 2].reshape(128, LANES))
        if i < 2:
            rows = rows + dot(move, other[:, i].reshape(128, LANES))
        b_kv[i] = rows.astype(BF)
        send(2 + i, b_kv.at[i], out)
    for copy in copies:
        copy.wait()


def on_device(
    prefix_query_rows,
    prefix_key_rows,
    prefix_value_rows,
    prefix_output_gradient,
    resp_q,
    resp_k,
    response_value_rows,
    response_output_gradient,
    lengths,
    prefix_order,
):
    vm = pltpu.VMEM
    dma = pltpu.SemaphoreType.DMA
    out = jax.ShapeDtypeStruct
    dqp, dqr, own, other = pl.pallas_call(
        kernel,
        out_shape=(
            out((8, 64, LANES), BF),
            out((8, 128, LANES), BF),
            out((8, 2, 2, 16, LANES), BF),
            out((8, 2, 16, LANES), BF),
        ),
        in_specs=[pl.BlockSpec(memory_space=pltpu.HBM)] * 10,
        out_specs=[pl.BlockSpec(memory_space=pl.ANY)] * 4,
        scratch_shapes=[
            pltpu.SMEM((16,), I32),
            pltpu.SMEM((2,), I32),
            vm((4, 2048, LANES), BF),
            vm((NQ, LANES), BF),
            vm((NQ, LANES), BF),
            vm((LANES, NQ), BF),
            vm((LANES, NQ), BF),
            vm((8, NQ), F32),
            vm((8, NQ), F32),
            vm((8, NQ), F32),
            vm((1, NQ), F32),
            vm((1, NQ), F32),
            vm((LANES, NQ), F32),
            vm((128, TW), I32),
            vm((128, TW), I32),
            vm((2048, NQ), F32),
            vm((2048, NQ), F32),
            vm((2048, NR), F32),
            vm((2048, NR), F32),
            vm((2, 2, 2, 2, 128, LANES), F32),
            vm((8, 2, 2, 128, LANES), BF),
            vm((8, 2, 2, 128, LANES), BF),
            vm((7, 2, 2, 128, LANES), BF),
            vm((3, 2, 2, 128, LANES), BF),
            vm((3, 2, 2, 128, LANES), BF),
            vm((2, 2, 128, LANES), BF),
            vm((2, 2, 128, LANES), BF),
            vm((NQ, LANES), BF),
            dma((10,)),
            dma((4, 16)),
            dma,
            dma,
            dma,
            dma((8, 2)),
            dma,
            dma((3, 2, 2)),
            dma((3, 2, 2)),
            dma((2, 2)),
            dma((4,)),
            dma((4,)),
            dma((3,)),
        ],
        compiler_params=pltpu.CompilerParams(
            collective_id=0, has_side_effects=True, vmem_limit_bytes=56 << 20
        ),
    )(
        prefix_order,
        lengths,
        prefix_query_rows.reshape(NP, LANES),
        prefix_output_gradient.reshape(NP, LANES),
        resp_q.reshape(NR, LANES),
        response_output_gradient.reshape(NR, LANES),
        prefix_key_rows.reshape(128, LANES),
        prefix_value_rows.reshape(128, LANES),
        resp_k.reshape(128, LANES),
        response_value_rows.reshape(128, LANES),
    )
    any_space = pl.BlockSpec(memory_space=pl.ANY)
    return pl.pallas_call(
        place,
        out_shape=(
            out((16, 8, 4, LANES), BF),
            out((128, LANES), BF),
            out((128, LANES), BF),
            out((16, 8, 8, LANES), BF),
            out((128, LANES), BF),
            out((128, LANES), BF),
        ),
        in_specs=[any_space] * 4,
        out_specs=[any_space] * 6,
        scratch_shapes=[
            vm((8, 16, 4, LANES), BF),
            vm((8, 16, 8, LANES), BF),
            vm((8, 2, 2, 16, LANES), BF),
            vm((8, 2, 16, LANES), BF),
            vm((16, 8, 4, LANES), BF),
            vm((16, 8, 8, LANES), BF),
            vm((4, 128, LANES), BF),
            dma((4,)),
            dma((6,)),
        ],
    )(
        dqp.reshape(8, 16, 4, LANES),
        dqr.reshape(8, 16, 8, LANES),
        own,
        other,
    )


def shaped(*args):
    pq, pk, pv, rq, rk, rv = on_device(*args)
    keys = (16, 8, LANES)
    return (
        pq, pk.reshape(keys), pv.reshape(keys),
        rq[None], rk.reshape(keys)[None], rv.reshape(keys)[None],
    )


def solution(mesh):
    in_specs = (
        P("blk", "head", "pair", None),
        P("blk", "head", None),
        P("blk", "head", None),
        P("blk", "head", "pair", None),
        P("pair", "blk", "head", None, None),
        P("pair", "blk", "head", None),
        P("pair", "blk", "head", None),
        P("pair", "blk", "head", None, None),
        P(),
        P(),
    )
    out_specs = (
        P(("blk", "head"), None, "pair", None),
        P(("blk", "head"), None, None),
        P(("blk", "head"), None, None),
        P("pair", ("blk", "head"), None, None, None),
        P("pair", ("blk", "head"), None, None),
        P("pair", ("blk", "head"), None, None),
    )
    return jax.shard_map(
        shaped, mesh=mesh, in_specs=in_specs, out_specs=out_specs, check_vma=False
    )
```

```python
import functools

import jax
import jax.numpy as jnp
from jax import lax
from jax.experimental import pallas as pl
from jax.experimental.pallas import tpu as pltpu
from jax.sharding import PartitionSpec as P

MESH = pl.DeviceIdType.MESH
F32 = jnp.float32
BF = jnp.bfloat16
I32 = jnp.int32
LANES = 128
SCALE = LANES ** -0.5
C = SCALE * 1.4426950408889634
LOW = -1e30
TW = 512
GW = 256
NP = 512
NR = 1024
NQ = NP + NR


def dot(a, b):
    return lax.dot_general(a, b, (((1,), (0,)), ((), ())), preferred_element_type=F32)


def masked(s, diff, t0, t1, fill):
    n = s.shape[0] // 2
    return jnp.concatenate(
        [jnp.where(diff <= t0, s[:n], fill), jnp.where(diff <= t1, s[n:], fill)], axis=0
    )


def kernel(
    order_in, lengths_in, pq, pdo, rq, rdo, pk, pv, rk, rv,
    o_dqp, o_dqr, o_own, o_other,
    order, lengths,
    kv, q, do, q_t, do_t, m, l, d, lse, dl, dq_t, diff_p, diff_r,
    s_pre, dp_pre, s_res, dp_res,
    acc, sib_out, sib_in, ring_out, l_in, r_in, far_in, fin,
    in_sem, ag_recv, ag_ring_send, ag_sib_send,
    rs_sib_send, rs_sib_recv, rs_send, l_recv, r_recv, far_recv,
    end_send, end_recv, loc_sem,
):
    b = lax.axis_index("blk")
    pair = lax.axis_index("pair")
    head = lax.axis_index("head")
    z = b // 2
    c = b % 2
    sib = b + 1 - 2 * c
    right = lax.rem(b + 2, 16)
    left = lax.rem(b + 14, 16)
    right2 = lax.rem(b + 4, 16)
    left2 = lax.rem(b + 12, 16)

    def rows_of(block):
        return pl.ds(pl.multiple_of(block * 128, 128), 128)

    loads = [
        pltpu.make_async_copy(ref, kv.at[i, rows_of(b), :], in_sem.at[i])
        for i, ref in enumerate((pk, pv, rk, rv))
    ] + [
        pltpu.make_async_copy(ref, dst, in_sem.at[4 + i])
        for i, (ref, dst) in enumerate((
            (pq, q.at[pl.ds(0, NP), :]),
            (rq, q.at[pl.ds(NP, NR), :]),
            (pdo, do.at[pl.ds(0, NP), :]),
            (rdo, do.at[pl.ds(NP, NR), :]),
            (order_in, order),
            (lengths_in, lengths),
        ))
    ]
    barrier = pltpu.get_barrier_semaphore()
    for n in (sib, right, left, right2, left2):
        pl.semaphore_signal(barrier, inc=1, device_id={"blk": n}, device_id_type=MESH)
    for k in range(1, 8):
        pl.semaphore_signal(
            barrier, inc=1, device_id={"head": lax.rem(head + k, 8)}, device_id_type=MESH
        )
    for k in range(8):
        pl.semaphore_signal(
            barrier, inc=1, device_id={"pair": 1 - pair, "head": lax.rem(head + k, 8)},
            device_id_type=MESH,
        )

    for copy in loads:
        copy.start()

    def kv_copy(i, block, send_sem, target):
        piece = kv.at[pl.ds(2 * i, 2), rows_of(block), :]
        return pltpu.make_async_remote_copy(
            src_ref=piece, dst_ref=piece, send_sem=send_sem, recv_sem=ag_recv.at[i, block],
            device_id={"blk": target}, device_id_type=MESH,
        )

    for copy in loads[:4]:
        copy.wait()
    pl.semaphore_wait(barrier, 20)
    for i in range(2):
        kv_copy(i, b, ag_ring_send, right).start()
        kv_copy(i, b, ag_ring_send, left).start()
        kv_copy(i, b, ag_sib_send, sib).start()

    for copy in loads[4:]:
        copy.wait()
    live = b * 128 < lengths[pair]
    do[NP:, :] = jnp.where(live, do[NP:, :].astype(F32), 0.0).astype(BF)
    q_t[...] = q[...].T
    do_t[...] = do[...].T
    m[...] = jnp.full(m.shape, LOW, F32)
    l[...] = jnp.zeros(l.shape, F32)
    d[...] = jnp.zeros(d.shape, F32)
    dq_t[...] = jnp.zeros(dq_t.shape, F32)
    key_row = lax.broadcasted_iota(I32, (128, TW), 0)
    column = lax.broadcasted_iota(I32, (128, TW), 1)
    diff_p[...] = key_row - column // 4
    diff_r[...] = key_row - column // 8

    def thresholds(zp, h, tile):
        if h == 0:
            if tile > 0:
                return ()
            own = order[b]
            return (diff_p[...], (own - order[2 * zp]) * 128, (own - order[2 * zp + 1]) * 128)
        t0 = (b - 2 * zp) * 128 + (tile - 1) * (TW // 8)
        return (diff_r[...], t0, t0 - 128)

    def keys_of(zp, h):
        rows = pl.ds(pl.multiple_of(zp * 256, 256), 256)
        return kv[2 * h, rows, :], kv[2 * h + 1, rows, :]

    stored = ((s_pre, dp_pre), (s_res, dp_res))

    def totals_unit(zp, h):
        k, v = keys_of(zp, h)
        rows = pl.ds(pl.multiple_of(zp * 256, 256), 256)
        for tile in range(h, NQ // TW):
            cs = pl.ds(tile * TW, TW)
            s = dot(k, q_t[:, cs]) * C
            dp = dot(v, do_t[:, cs])
            limits = thresholds(zp, h, tile)
            if limits:
                s = masked(s, *limits, LOW)
            there = pl.ds((tile - h) * TW, TW)
            stored[h][0][rows, there] = s
            stored[h][1][rows, there] = dp
            s = s.reshape(-1, 8, TW)
            dp = dp.reshape(-1, 8, TW)
            old = m[:, cs]
            new = jnp.maximum(old, jnp.max(s, axis=0))
            e = jnp.exp2(s - new[None])
            shrink = jnp.exp2(old - new)
            m[:, cs] = new
            l[:, cs] = l[:, cs] * shrink + jnp.sum(e, axis=0)
            d[:, cs] = d[:, cs] * shrink + jnp.sum(e * dp, axis=0)

    def take_ring(k):
        from_left = lax.rem(b + 16 - 2 * k, 16)
        from_right = lax.rem(b + 2 * k, 16)

        def take(i, block, target, go_on):
            kv_copy(i, block, ag_ring_send, target).wait_recv()

            @pl.when(go_on)
            def _():
                kv_copy(i, block, ag_ring_send, target).start()

            kv_copy(i, block, ag_sib_send, sib).start()

        for i in range(2):
            there = i == 0

            @pl.when((k < 4) | there)
            def _():
                take(i, from_left, right, (k < 3) | ((k == 3) & there))

            @pl.when((k < 4) | (not there))
            def _():
                take(i, from_right, left, (k < 3) | ((k == 3) & (not there)))

    def totals_step(n, carry):
        @pl.when((n == 0) | (n == 1) | (n == 3) | (n == 7))
        def _():
            take_ring(jnp.where(n == 0, 1, jnp.where(n == 7, 4, (n + 3) // 2)))

        k = (n + 1) // 2
        zp = lax.rem(jnp.where(n % 2 == 1, z + 8 - k, z + k), 8)
        for i in range(2):
            kv_copy(i, 2 * zp + 1 - c, ag_sib_send, sib).wait_recv()
        totals_unit(zp, 0)

        @pl.when(zp <= z)
        def _():
            totals_unit(zp, 1)

        return carry

    lax.fori_loop(0, 8, totals_step, 0)

    top = jnp.max(m[...], axis=0, keepdims=True)
    weight = jnp.exp2(m[...] - top)
    total = jnp.sum(l[...] * weight, axis=0, keepdims=True)
    lse[...] = top + jnp.log2(total)
    dl[...] = jnp.sum(d[...] * weight, axis=0, keepdims=True) / total

    def grads_unit(zp, h, slot):
        rows = pl.ds(pl.multiple_of(zp * 256, 256), 256)
        k_t = kv[2 * h, rows, :].T
        dk = jnp.zeros((256, LANES), F32)
        dv = jnp.zeros((256, LANES), F32)
        for tile in range((NQ - h * NP) // GW):
            there = pl.ds(tile * GW, GW)
            cs = pl.ds(h * NP + tile * GW, GW)
            p = jnp.exp2(stored[h][0][rows, there] - lse[:, cs])
            ds = (p * (stored[h][1][rows, there] - dl[:, cs]) * SCALE).astype(BF)
            dk += dot(ds, q[cs, :])
            dv += dot(p.astype(BF), do[cs, :])
            dq_t[:, cs] += dot(k_t, ds)
        for i, part in ((0, dk), (1, dv)):
            acc[slot, h, 0, i] = part[:128]
            acc[slot, h, 1, i] = part[128:]

    def sib_copy(t, h):
        return pltpu.make_async_remote_copy(
            src_ref=sib_out.at[t, h], dst_ref=sib_in.at[t, h], send_sem=rs_sib_send,
            recv_sem=rs_sib_recv.at[t, h], device_id={"blk": sib}, device_id_type=MESH,
        )

    def left_copy(k, h):
        return pltpu.make_async_remote_copy(
            src_ref=ring_out.at[k - 1, h], dst_ref=l_in.at[k - 1, h],
            send_sem=rs_send, recv_sem=l_recv.at[k - 1, h],
            device_id={"blk": left}, device_id_type=MESH,
        )

    def right_copy(k, h):
        return pltpu.make_async_remote_copy(
            src_ref=ring_out.at[k + 2, h], dst_ref=r_in.at[k - 1, h],
            send_sem=rs_send, recv_sem=r_recv.at[k - 1, h],
            device_id={"blk": right}, device_id_type=MESH,
        )

    def far_copy(h):
        return pltpu.make_async_remote_copy(
            src_ref=ring_out.at[6, h], dst_ref=far_in.at[h],
            send_sem=rs_send, recv_sem=far_recv.at[h],
            device_id={"blk": (left2, right2)[h]}, device_id_type=MESH,
        )

    def compute(t, h):
        k = jnp.where(t == 0, 4, 3 - (t - 1) // 2)
        zp = lax.rem(jnp.where(t % 2 == 1, z + 8 - k, z + k), 8)
        slot = t % 2
        if h == 0:
            grads_unit(zp, 0, slot)
        else:
            @pl.when(zp <= z)
            def _():
                grads_unit(zp, 1, slot)

            @pl.when(zp > z)
            def _():
                acc[slot, 1] = jnp.zeros(acc.shape[2:], F32)

        sib_out[t, h] = acc[slot, h, 1 - c].astype(BF)
        sib_copy(t, h).start()

    def finalize(t, h):
        k = 3 - (t - 1) // 2
        slot = t % 2
        sib_copy(t, h).wait_recv()
        part = acc[slot, h, c] + sib_in[t, h].astype(F32)

        def pass_on(place_of, copy_of, into, with_far):
            @pl.when(k == 3)
            def _():
                ring_out[place_of, h] = part.astype(BF)

            @pl.when(k < 3)
            def _():
                copy_of(k + 1, h).wait_recv()
                acc[slot, h, c] = part + into[k, h].astype(F32)
                if with_far:
                    @pl.when(k == 2)
                    def _():
                        far_copy(h).wait_recv()
                        acc[slot, h, c] = acc[slot, h, c] + far_in[h].astype(F32)

                ring_out[place_of, h] = acc[slot, h, c].astype(BF)

            copy_of(k, h).start()

        @pl.when(t == 0)
        def _():
            ring_out[6, h] = part.astype(BF)
            far_copy(h).start()

        @pl.when(t % 2 == 1)
        def _():
            pass_on(k - 1, left_copy, l_in, h == 0)

        @pl.when((t % 2 == 0) & (t > 0))
        def _():
            pass_on(k + 2, right_copy, r_in, h == 1)

    def grads_step(t, carry):
        for h in range(2):
            compute(t, h)

            @pl.when(t > 0)
            def _():
                finalize(t - 1, h)

        return carry

    lax.fori_loop(0, 8, grads_step, 0)

    def peer(k, other):
        where = {"head": lax.rem(head + k, 8)}
        if other:
            where["pair"] = 1 - pair
        return where

    def to_heads(k, src, dst, send_sem, recv_sem, other=False):
        return pltpu.make_async_remote_copy(
            src_ref=src, dst_ref=dst, send_sem=send_sem, recv_sem=recv_sem,
            device_id=peer(k, other), device_id_type=MESH,
        )

    def dq_copies(k):
        h = lax.rem(head + k, 8)
        rows_p = q.at[pl.ds(pl.multiple_of(h * 64, 64), 64), :]
        rows_r = q.at[pl.ds(pl.multiple_of(NP + h * 128, 128), 128), :]
        return ((rows_p, o_dqp.at[head]), (rows_r, o_dqr.at[head]))

    def kv_rows(k):
        return pl.ds(pl.multiple_of(lax.rem(head + k, 8) * 16, 16), 16)

    q[...] = dq_t[...].T.astype(BF)
    local = []
    for k in range(1, 8):
        for i, (src, dst) in enumerate(dq_copies(k)):
            to_heads(k, src, dst, end_send.at[i], end_recv.at[i]).start()
    for i, (src, dst) in enumerate(dq_copies(0)):
        copy = pltpu.make_async_copy(src, dst, loc_sem.at[i])
        copy.start()
        local.append(copy)

    for h in range(2):
        sib_copy(7, h).wait_recv()
        part = acc[1, h, c] + sib_in[7, h].astype(F32)
        left_copy(1, h).wait_recv()
        right_copy(1, h).wait_recv()
        fin[h] = (part + l_in[0, h].astype(F32) + r_in[0, h].astype(F32)).astype(BF)
        if h == 0:
            for k in range(8):
                to_heads(
                    k, fin.at[0, :, kv_rows(k), :], o_other.at[head], end_send.at[3],
                    end_recv.at[3], other=True,
                ).start()
        for k in range(1, 8):
            to_heads(
                k, fin.at[h, :, kv_rows(k), :], o_own.at[head, h], end_send.at[2], end_recv.at[2]
            ).start()
    copy = pltpu.make_async_copy(fin.at[:, :, kv_rows(0), :], o_own.at[head], loc_sem.at[2])
    copy.start()
    local.append(copy)

    def wait_sends(ref, sem):
        pltpu.make_async_copy(ref, ref, sem).wait()

    wait_sends(kv.at[:, pl.ds(0, 7 * 128), :], ag_ring_send)
    wait_sends(kv.at[:, pl.ds(0, 8 * 128), :], ag_sib_send)
    wait_sends(sib_out, rs_sib_send)
    wait_sends(ring_out, rs_send)
    wait_sends(q.at[pl.ds(0, 7 * 64), :], end_send.at[0])
    wait_sends(q.at[pl.ds(0, 7 * 128), :], end_send.at[1])
    wait_sends(fin.at[:, :, pl.ds(0, 7 * 16), :], end_send.at[2])
    wait_sends(fin.at[0], end_send.at[3])
    for copy in local:
        copy.wait()
    for sem, ref in enumerate((o_dqp, o_dqr, o_own)):
        wait_sends(ref.at[pl.ds(0, 7)], end_recv.at[sem])
    wait_sends(o_other, end_recv.at[3])


def place(
    i_dqp, i_dqr, i_own, i_other, o_pq, o_pk, o_pv, o_rq, o_rk, o_rv,
    dqp, dqr, own, other, b_pq, b_rq, b_kv, in_sems, sems,
):
    loads = [
        pltpu.make_async_copy(src, dst, in_sems.at[i])
        for i, (src, dst) in enumerate(((i_dqp, dqp), (i_dqr, dqr), (i_own, own), (i_other, other)))
    ]
    for load in loads:
        load.start()
    copies = []

    def send(i, src, dst):
        copy = pltpu.make_async_copy(src, dst, sems.at[i])
        copy.start()
        copies.append(copy)

    loads[1].wait()
    for g in range(8):
        b_rq[:, g] = dqr[g]
    send(0, b_rq, o_rq)
    loads[0].wait()
    for g in range(8):
        b_pq[:, g] = dqp[g]
    send(1, b_pq, o_pq)
    to = lax.broadcasted_iota(I32, (128, 128), 0)
    source = lax.broadcasted_iota(I32, (128, 128), 1)
    move = jnp.where(source == (to % 8) * 16 + to // 8, 1.0, 0.0).astype(BF)
    loads[2].wait()
    loads[3].wait()
    for i, out in enumerate((o_pk, o_pv, o_rk, o_rv)):
        rows = dot(move, own[:, i // 2, i % 2].reshape(128, LANES))
        if i < 2:
            rows = rows + dot(move, other[:, i].reshape(128, LANES))
        b_kv[i] = rows.astype(BF)
        send(2 + i, b_kv.at[i], out)
    for copy in copies:
        copy.wait()


def on_device(
    prefix_query_rows,
    prefix_key_rows,
    prefix_value_rows,
    prefix_output_gradient,
    resp_q,
    resp_k,
    response_value_rows,
    response_output_gradient,
    lengths,
    prefix_order,
):
    vm = pltpu.VMEM
    dma = pltpu.SemaphoreType.DMA
    out = jax.ShapeDtypeStruct
    dqp, dqr, own, other = pl.pallas_call(
        kernel,
        out_shape=(
            out((8, 64, LANES), BF),
            out((8, 128, LANES), BF),
            out((8, 2, 2, 16, LANES), BF),
            out((8, 2, 16, LANES), BF),
        ),
        in_specs=[pl.BlockSpec(memory_space=pltpu.HBM)] * 10,
        out_specs=[pl.BlockSpec(memory_space=pl.ANY)] * 4,
        scratch_shapes=[
            pltpu.SMEM((16,), I32),
            pltpu.SMEM((2,), I32),
            vm((4, 2048, LANES), BF),
            vm((NQ, LANES), BF),
            vm((NQ, LANES), BF),
            vm((LANES, NQ), BF),
            vm((LANES, NQ), BF),
            vm((8, NQ), F32),
            vm((8, NQ), F32),
            vm((8, NQ), F32),
            vm((1, NQ), F32),
            vm((1, NQ), F32),
            vm((LANES, NQ), F32),
            vm((128, TW), I32),
            vm((128, TW), I32),
            vm((2048, NQ), F32),
            vm((2048, NQ), F32),
            vm((2048, NR), F32),
            vm((2048, NR), F32),
            vm((2, 2, 2, 2, 128, LANES), F32),
            vm((8, 2, 2, 128, LANES), BF),
            vm((8, 2, 2, 128, LANES), BF),
            vm((7, 2, 2, 128, LANES), BF),
            vm((3, 2, 2, 128, LANES), BF),
            vm((3, 2, 2, 128, LANES), BF),
            vm((2, 2, 128, LANES), BF),
            vm((2, 2, 128, LANES), BF),
            dma((10,)),
            dma((2, 16)),
            dma,
            dma,
            dma,
            dma((8, 2)),
            dma,
            dma((3, 2)),
            dma((3, 2)),
            dma((2,)),
            dma((4,)),
            dma((4,)),
            dma((3,)),
        ],
        compiler_params=pltpu.CompilerParams(
            collective_id=0, has_side_effects=True, vmem_limit_bytes=52 << 20
        ),
    )(
        prefix_order,
        lengths,
        prefix_query_rows.reshape(NP, LANES),
        prefix_output_gradient.reshape(NP, LANES),
        resp_q.reshape(NR, LANES),
        response_output_gradient.reshape(NR, LANES),
        prefix_key_rows.reshape(128, LANES),
        prefix_value_rows.reshape(128, LANES),
        resp_k.reshape(128, LANES),
        response_value_rows.reshape(128, LANES),
    )
    any_space = pl.BlockSpec(memory_space=pl.ANY)
    return pl.pallas_call(
        place,
        out_shape=(
            out((16, 8, 4, LANES), BF),
            out((128, LANES), BF),
            out((128, LANES), BF),
            out((16, 8, 8, LANES), BF),
            out((128, LANES), BF),
            out((128, LANES), BF),
        ),
        in_specs=[any_space] * 4,
        out_specs=[any_space] * 6,
        scratch_shapes=[
            vm((8, 16, 4, LANES), BF),
            vm((8, 16, 8, LANES), BF),
            vm((8, 2, 2, 16, LANES), BF),
            vm((8, 2, 16, LANES), BF),
            vm((16, 8, 4, LANES), BF),
            vm((16, 8, 8, LANES), BF),
            vm((4, 128, LANES), BF),
            dma((4,)),
            dma((6,)),
        ],
    )(
        dqp.reshape(8, 16, 4, LANES),
        dqr.reshape(8, 16, 8, LANES),
        own,
        other,
    )


def shaped(*args):
    pq, pk, pv, rq, rk, rv = on_device(*args)
    keys = (16, 8, LANES)
    return (
        pq, pk.reshape(keys), pv.reshape(keys),
        rq[None], rk.reshape(keys)[None], rv.reshape(keys)[None],
    )


def solution(mesh):
    in_specs = (
        P("blk", "head", "pair", None),
        P("blk", "head", None),
        P("blk", "head", None),
        P("blk", "head", "pair", None),
        P("pair", "blk", "head", None, None),
        P("pair", "blk", "head", None),
        P("pair", "blk", "head", None),
        P("pair", "blk", "head", None, None),
        P(),
        P(),
    )
    out_specs = (
        P(("blk", "head"), None, "pair", None),
        P(("blk", "head"), None, None),
        P(("blk", "head"), None, None),
        P("pair", ("blk", "head"), None, None, None),
        P("pair", ("blk", "head"), None, None),
        P("pair", ("blk", "head"), None, None),
    )
    return jax.shard_map(
        shaped, mesh=mesh, in_specs=in_specs, out_specs=out_specs, check_vma=False
    )
```

```python
import functools

import jax
import jax.numpy as jnp
from jax import lax
from jax.experimental import pallas as pl
from jax.experimental.pallas import tpu as pltpu
from jax.sharding import PartitionSpec as P

MESH = pl.DeviceIdType.MESH
F32 = jnp.float32
BF = jnp.bfloat16
I32 = jnp.int32
LANES = 128
SCALE = LANES ** -0.5
C = SCALE * 1.4426950408889634
LOW = -1e30
TW = 512
GW = 256
NP = 512
NR = 1024
NQ = NP + NR


def dot(a, b):
    return lax.dot_general(a, b, (((1,), (0,)), ((), ())), preferred_element_type=F32)


def masked(s, diff, t0, t1, fill):
    n = s.shape[0] // 2
    return jnp.concatenate(
        [jnp.where(diff <= t0, s[:n], fill), jnp.where(diff <= t1, s[n:], fill)], axis=0
    )


def kernel(
    order_in, lengths_in, pq, pdo, rq, rdo, pk, pv, rk, rv,
    o_dqp, o_dqr, o_own, o_other,
    order, lengths,
    kv, q, do, q_t, do_t, m, l, d, lse, dl, dq_t, diff_p, diff_r,
    s_pre, dp_pre, s_res, dp_res,
    acc, sib_out, sib_in, ring_out, l_in, r_in, far_in, fin, dq,
    in_sem, ag_recv, ag_ring_send, ag_sib_send,
    rs_sib_send, rs_sib_recv, rs_send, l_recv, r_recv, far_recv,
    end_send, end_recv, loc_sem,
):
    b = lax.axis_index("blk")
    pair = lax.axis_index("pair")
    head = lax.axis_index("head")
    z = b // 2
    c = b % 2
    sib = b + 1 - 2 * c
    right = lax.rem(b + 2, 16)
    left = lax.rem(b + 14, 16)
    right2 = lax.rem(b + 4, 16)
    left2 = lax.rem(b + 12, 16)

    def rows_of(block):
        return pl.ds(pl.multiple_of(block * 128, 128), 128)

    loads = [
        pltpu.make_async_copy(ref, kv.at[i, rows_of(b), :], in_sem.at[i])
        for i, ref in enumerate((pk, pv, rk, rv))
    ] + [
        pltpu.make_async_copy(ref, dst, in_sem.at[4 + i])
        for i, (ref, dst) in enumerate((
            (pq, q.at[pl.ds(0, NP), :]),
            (rq, q.at[pl.ds(NP, NR), :]),
            (pdo, do.at[pl.ds(0, NP), :]),
            (rdo, do.at[pl.ds(NP, NR), :]),
            (order_in, order),
            (lengths_in, lengths),
        ))
    ]
    barrier = pltpu.get_barrier_semaphore()
    for n in (sib, right, left, right2, left2):
        pl.semaphore_signal(barrier, inc=1, device_id={"blk": n}, device_id_type=MESH)
    for k in range(1, 8):
        pl.semaphore_signal(
            barrier, inc=1, device_id={"head": lax.rem(head + k, 8)}, device_id_type=MESH
        )
    for k in range(8):
        pl.semaphore_signal(
            barrier, inc=1, device_id={"pair": 1 - pair, "head": lax.rem(head + k, 8)},
            device_id_type=MESH,
        )

    for copy in loads:
        copy.start()

    def kv_copy(i, block, send_sem, target):
        piece = kv.at[i, rows_of(block), :]
        return pltpu.make_async_remote_copy(
            src_ref=piece, dst_ref=piece, send_sem=send_sem, recv_sem=ag_recv.at[i, block],
            device_id={"blk": target}, device_id_type=MESH,
        )

    for copy in loads[:4]:
        copy.wait()
    pl.semaphore_wait(barrier, 20)
    for i in range(4):
        kv_copy(i, b, ag_ring_send, right).start()
        kv_copy(i, b, ag_ring_send, left).start()
        kv_copy(i, b, ag_sib_send, sib).start()

    for copy in loads[4:]:
        copy.wait()
    live = b * 128 < lengths[pair]
    do[NP:, :] = jnp.where(live, do[NP:, :].astype(F32), 0.0).astype(BF)
    q_t[...] = q[...].T
    do_t[...] = do[...].T
    m[...] = jnp.full(m.shape, LOW, F32)
    l[...] = jnp.zeros(l.shape, F32)
    d[...] = jnp.zeros(d.shape, F32)
    dq_t[...] = jnp.zeros(dq_t.shape, F32)
    key_row = lax.broadcasted_iota(I32, (128, TW), 0)
    column = lax.broadcasted_iota(I32, (128, TW), 1)
    diff_p[...] = key_row - column // 4
    diff_r[...] = key_row - column // 8

    def thresholds(zp, h, tile):
        if h == 0:
            if tile > 0:
                return ()
            own = order[b]
            return (diff_p[...], (own - order[2 * zp]) * 128, (own - order[2 * zp + 1]) * 128)
        t0 = (b - 2 * zp) * 128 + (tile - 1) * (TW // 8)
        return (diff_r[...], t0, t0 - 128)

    def keys_of(zp, h):
        rows = pl.ds(pl.multiple_of(zp * 256, 256), 256)
        return kv[2 * h, rows, :], kv[2 * h + 1, rows, :]

    stored = ((s_pre, dp_pre), (s_res, dp_res))

    def totals_unit(zp, h):
        k, v = keys_of(zp, h)
        rows = pl.ds(pl.multiple_of(zp * 256, 256), 256)
        for tile in range(h, NQ // TW):
            cs = pl.ds(tile * TW, TW)
            s = dot(k, q_t[:, cs]) * C
            dp = dot(v, do_t[:, cs])
            limits = thresholds(zp, h, tile)
            if limits:
                s = masked(s, *limits, LOW)
            there = pl.ds((tile - h) * TW, TW)
            stored[h][0][rows, there] = s
            stored[h][1][rows, there] = dp
            s = s.reshape(-1, 8, TW)
            dp = dp.reshape(-1, 8, TW)
            old = m[:, cs]
            new = jnp.maximum(old, jnp.max(s, axis=0))
            e = jnp.exp2(s - new[None])
            shrink = jnp.exp2(old - new)
            m[:, cs] = new
            l[:, cs] = l[:, cs] * shrink + jnp.sum(e, axis=0)
            d[:, cs] = d[:, cs] * shrink + jnp.sum(e * dp, axis=0)

    def take_ring(k):
        from_left = lax.rem(b + 16 - 2 * k, 16)
        from_right = lax.rem(b + 2 * k, 16)

        def take(i, block, target, go_on):
            kv_copy(i, block, ag_ring_send, target).wait_recv()

            @pl.when(go_on)
            def _():
                kv_copy(i, block, ag_ring_send, target).start()

            kv_copy(i, block, ag_sib_send, sib).start()

        for i in range(4):
            there = i < 2

            @pl.when((k < 4) | there)
            def _():
                take(i, from_left, right, (k < 3) | ((k == 3) & there))

            @pl.when((k < 4) | (not there))
            def _():
                take(i, from_right, left, (k < 3) | ((k == 3) & (not there)))

    def totals_step(n, carry):
        @pl.when((n == 0) | (n == 1) | (n == 3) | (n == 7))
        def _():
            take_ring(jnp.where(n == 0, 1, jnp.where(n == 7, 4, (n + 3) // 2)))

        k = (n + 1) // 2
        zp = lax.rem(jnp.where(n % 2 == 1, z + 8 - k, z + k), 8)
        for i in range(4):
            kv_copy(i, 2 * zp + 1 - c, ag_sib_send, sib).wait_recv()
        totals_unit(zp, 0)

        @pl.when(zp <= z)
        def _():
            totals_unit(zp, 1)

        return carry

    lax.fori_loop(0, 8, totals_step, 0)

    top = jnp.max(m[...], axis=0, keepdims=True)
    weight = jnp.exp2(m[...] - top)
    total = jnp.sum(l[...] * weight, axis=0, keepdims=True)
    lse[...] = top + jnp.log2(total)
    dl[...] = jnp.sum(d[...] * weight, axis=0, keepdims=True) / total

    def grads_unit(zp, h, slot):
        rows = pl.ds(pl.multiple_of(zp * 256, 256), 256)
        k_t = kv[2 * h, rows, :].T
        dk = jnp.zeros((256, LANES), F32)
        dv = jnp.zeros((256, LANES), F32)
        for tile in range((NQ - h * NP) // GW):
            there = pl.ds(tile * GW, GW)
            cs = pl.ds(h * NP + tile * GW, GW)
            p = jnp.exp2(stored[h][0][rows, there] - lse[:, cs])
            ds = (p * (stored[h][1][rows, there] - dl[:, cs]) * SCALE).astype(BF)
            dk += dot(ds, q[cs, :])
            dv += dot(p.astype(BF), do[cs, :])
            dq_t[:, cs] += dot(k_t, ds)
        for i, part in ((0, dk), (1, dv)):
            acc[slot, h, 0, i] = part[:128]
            acc[slot, h, 1, i] = part[128:]

    def sib_copy(t, h):
        return pltpu.make_async_remote_copy(
            src_ref=sib_out.at[t, h], dst_ref=sib_in.at[t, h], send_sem=rs_sib_send,
            recv_sem=rs_sib_recv.at[t, h], device_id={"blk": sib}, device_id_type=MESH,
        )

    def left_copy(k, h, i):
        return pltpu.make_async_remote_copy(
            src_ref=ring_out.at[k - 1, h, i], dst_ref=l_in.at[k - 1, h, i],
            send_sem=rs_send, recv_sem=l_recv.at[k - 1, h, i],
            device_id={"blk": left}, device_id_type=MESH,
        )

    def right_copy(k, h, i):
        return pltpu.make_async_remote_copy(
            src_ref=ring_out.at[k + 2, h, i], dst_ref=r_in.at[k - 1, h, i],
            send_sem=rs_send, recv_sem=r_recv.at[k - 1, h, i],
            device_id={"blk": right}, device_id_type=MESH,
        )

    def far_copy(h, i):
        return pltpu.make_async_remote_copy(
            src_ref=ring_out.at[6, h, i], dst_ref=far_in.at[h, i],
            send_sem=rs_send, recv_sem=far_recv.at[h, i],
            device_id={"blk": (left2, right2)[h]}, device_id_type=MESH,
        )

    def compute(t, h):
        k = jnp.where(t == 0, 4, 3 - (t - 1) // 2)
        zp = lax.rem(jnp.where(t % 2 == 1, z + 8 - k, z + k), 8)
        slot = t % 2
        if h == 0:
            grads_unit(zp, 0, slot)
        else:
            @pl.when(zp <= z)
            def _():
                grads_unit(zp, 1, slot)

            @pl.when(zp > z)
            def _():
                acc[slot, 1] = jnp.zeros(acc.shape[2:], F32)

        sib_out[t, h] = acc[slot, h, 1 - c].astype(BF)
        sib_copy(t, h).start()

    def finalize(t, h):
        k = 3 - (t - 1) // 2
        slot = t % 2
        sib_copy(t, h).wait_recv()
        for i in range(2):
            acc[slot, h, c, i] = acc[slot, h, c, i] + sib_in[t, h, i].astype(F32)

        def pass_on(place_of, copy_of, into, with_far):
            for i in range(2):
                @pl.when(k < 3)
                def _():
                    copy_of(k + 1, h, i).wait_recv()
                    acc[slot, h, c, i] = acc[slot, h, c, i] + into[k, h, i].astype(F32)

                if with_far:
                    @pl.when(k == 2)
                    def _():
                        far_copy(h, i).wait_recv()
                        acc[slot, h, c, i] = acc[slot, h, c, i] + far_in[h, i].astype(F32)

                ring_out[place_of, h, i] = acc[slot, h, c, i].astype(BF)
                copy_of(k, h, i).start()

        @pl.when(t == 0)
        def _():
            for i in range(2):
                ring_out[6, h, i] = acc[slot, h, c, i].astype(BF)
                far_copy(h, i).start()

        @pl.when(t % 2 == 1)
        def _():
            pass_on(k - 1, left_copy, l_in, h == 0)

        @pl.when((t % 2 == 0) & (t > 0))
        def _():
            pass_on(k + 2, right_copy, r_in, h == 1)

    def grads_step(t, carry):
        for h in range(2):
            compute(t, h)

            @pl.when(t > 0)
            def _():
                finalize(t - 1, h)

        return carry

    lax.fori_loop(0, 8, grads_step, 0)

    def peer(k, other):
        where = {"head": lax.rem(head + k, 8)}
        if other:
            where["pair"] = 1 - pair
        return where

    def to_heads(k, src, dst, send_sem, recv_sem, other=False):
        return pltpu.make_async_remote_copy(
            src_ref=src, dst_ref=dst, send_sem=send_sem, recv_sem=recv_sem,
            device_id=peer(k, other), device_id_type=MESH,
        )

    def dq_copies(k):
        h = lax.rem(head + k, 8)
        rows_p = dq.at[pl.ds(pl.multiple_of(h * 64, 64), 64), :]
        rows_r = dq.at[pl.ds(pl.multiple_of(NP + h * 128, 128), 128), :]
        return ((rows_p, o_dqp.at[head]), (rows_r, o_dqr.at[head]))

    def kv_rows(k):
        return pl.ds(pl.multiple_of(lax.rem(head + k, 8) * 16, 16), 16)

    dq[...] = dq_t[...].T.astype(BF)
    local = []
    for k in range(1, 8):
        for i, (src, dst) in enumerate(dq_copies(k)):
            to_heads(k, src, dst, end_send.at[i], end_recv.at[i]).start()
    for i, (src, dst) in enumerate(dq_copies(0)):
        copy = pltpu.make_async_copy(src, dst, loc_sem.at[i])
        copy.start()
        local.append(copy)

    for h in range(2):
        sib_copy(7, h).wait_recv()
        for i in range(2):
            part = acc[1, h, c, i] + sib_in[7, h, i].astype(F32)
            left_copy(1, h, i).wait_recv()
            right_copy(1, h, i).wait_recv()
            part = part + l_in[0, h, i].astype(F32) + r_in[0, h, i].astype(F32)
            fin[h, i] = part.astype(BF)
        if h == 0:
            for k in range(8):
                to_heads(
                    k, fin.at[0, :, kv_rows(k), :], o_other.at[head], end_send.at[3],
                    end_recv.at[3], other=True,
                ).start()
        for k in range(1, 8):
            to_heads(
                k, fin.at[h, :, kv_rows(k), :], o_own.at[head, h], end_send.at[2], end_recv.at[2]
            ).start()
    copy = pltpu.make_async_copy(fin.at[:, :, kv_rows(0), :], o_own.at[head], loc_sem.at[2])
    copy.start()
    local.append(copy)

    def wait_sends(ref, sem):
        pltpu.make_async_copy(ref, ref, sem).wait()

    wait_sends(kv.at[:, pl.ds(0, 7 * 128), :], ag_ring_send)
    wait_sends(kv.at[:, pl.ds(0, 8 * 128), :], ag_sib_send)
    wait_sends(sib_out, rs_sib_send)
    wait_sends(ring_out, rs_send)
    wait_sends(dq.at[pl.ds(0, 7 * 64), :], end_send.at[0])
    wait_sends(dq.at[pl.ds(0, 7 * 128), :], end_send.at[1])
    wait_sends(fin.at[:, :, pl.ds(0, 7 * 16), :], end_send.at[2])
    wait_sends(fin.at[0], end_send.at[3])
    for copy in local:
        copy.wait()
    for sem, ref in enumerate((o_dqp, o_dqr, o_own)):
        wait_sends(ref.at[pl.ds(0, 7)], end_recv.at[sem])
    wait_sends(o_other, end_recv.at[3])


def place(
    i_dqp, i_dqr, i_own, i_other, o_pq, o_pk, o_pv, o_rq, o_rk, o_rv,
    dqp, dqr, own, other, b_pq, b_rq, b_kv, in_sems, sems,
):
    loads = [
        pltpu.make_async_copy(src, dst, in_sems.at[i])
        for i, (src, dst) in enumerate(((i_dqp, dqp), (i_dqr, dqr), (i_own, own), (i_other, other)))
    ]
    for load in loads:
        load.start()
    copies = []

    def send(i, src, dst):
        copy = pltpu.make_async_copy(src, dst, sems.at[i])
        copy.start()
        copies.append(copy)

    loads[1].wait()
    for g in range(8):
        b_rq[:, g] = dqr[g]
    send(0, b_rq, o_rq)
    loads[0].wait()
    for g in range(8):
        b_pq[:, g] = dqp[g]
    send(1, b_pq, o_pq)
    to = lax.broadcasted_iota(I32, (128, 128), 0)
    source = lax.broadcasted_iota(I32, (128, 128), 1)
    move = jnp.where(source == (to % 8) * 16 + to // 8, 1.0, 0.0).astype(BF)
    loads[2].wait()
    loads[3].wait()
    for i, out in enumerate((o_pk, o_pv, o_rk, o_rv)):
        rows = dot(move, own[:, i // 2, i % 2].reshape(128, LANES))
        if i < 2:
            rows = rows + dot(move, other[:, i].reshape(128, LANES))
        b_kv[i] = rows.astype(BF)
        send(2 + i, b_kv.at[i], out)
    for copy in copies:
        copy.wait()


def on_device(
    prefix_query_rows,
    prefix_key_rows,
    prefix_value_rows,
    prefix_output_gradient,
    resp_q,
    resp_k,
    response_value_rows,
    response_output_gradient,
    lengths,
    prefix_order,
):
    vm = pltpu.VMEM
    dma = pltpu.SemaphoreType.DMA
    out = jax.ShapeDtypeStruct
    dqp, dqr, own, other = pl.pallas_call(
        kernel,
        out_shape=(
            out((8, 64, LANES), BF),
            out((8, 128, LANES), BF),
            out((8, 2, 2, 16, LANES), BF),
            out((8, 2, 16, LANES), BF),
        ),
        in_specs=[pl.BlockSpec(memory_space=pltpu.HBM)] * 10,
        out_specs=[pl.BlockSpec(memory_space=pl.ANY)] * 4,
        scratch_shapes=[
            pltpu.SMEM((16,), I32),
            pltpu.SMEM((2,), I32),
            vm((4, 2048, LANES), BF),
            vm((NQ, LANES), BF),
            vm((NQ, LANES), BF),
            vm((LANES, NQ), BF),
            vm((LANES, NQ), BF),
            vm((8, NQ), F32),
            vm((8, NQ), F32),
            vm((8, NQ), F32),
            vm((1, NQ), F32),
            vm((1, NQ), F32),
            vm((LANES, NQ), F32),
            vm((128, TW), I32),
            vm((128, TW), I32),
            vm((2048, NQ), F32),
            vm((2048, NQ), F32),
            vm((2048, NR), F32),
            vm((2048, NR), F32),
            vm((2, 2, 2, 2, 128, LANES), F32),
            vm((8, 2, 2, 128, LANES), BF),
            vm((8, 2, 2, 128, LANES), BF),
            vm((7, 2, 2, 128, LANES), BF),
            vm((3, 2, 2, 128, LANES), BF),
            vm((3, 2, 2, 128, LANES), BF),
            vm((2, 2, 128, LANES), BF),
            vm((2, 2, 128, LANES), BF),
            vm((NQ, LANES), BF),
            dma((10,)),
            dma((4, 16)),
            dma,
            dma,
            dma,
            dma((8, 2)),
            dma,
            dma((3, 2, 2)),
            dma((3, 2, 2)),
            dma((2, 2)),
            dma((4,)),
            dma((4,)),
            dma((3,)),
        ],
        compiler_params=pltpu.CompilerParams(
            collective_id=0, has_side_effects=True, vmem_limit_bytes=56 << 20
        ),
    )(
        prefix_order,
        lengths,
        prefix_query_rows.reshape(NP, LANES),
        prefix_output_gradient.reshape(NP, LANES),
        resp_q.reshape(NR, LANES),
        response_output_gradient.reshape(NR, LANES),
        prefix_key_rows.reshape(128, LANES),
        prefix_value_rows.reshape(128, LANES),
        resp_k.reshape(128, LANES),
        response_value_rows.reshape(128, LANES),
    )
    any_space = pl.BlockSpec(memory_space=pl.ANY)
    return pl.pallas_call(
        place,
        out_shape=(
            out((16, 8, 4, LANES), BF),
            out((128, LANES), BF),
            out((128, LANES), BF),
            out((16, 8, 8, LANES), BF),
            out((128, LANES), BF),
            out((128, LANES), BF),
        ),
        in_specs=[any_space] * 4,
        out_specs=[any_space] * 6,
        scratch_shapes=[
            vm((8, 16, 4, LANES), BF),
            vm((8, 16, 8, LANES), BF),
            vm((8, 2, 2, 16, LANES), BF),
            vm((8, 2, 16, LANES), BF),
            vm((16, 8, 4, LANES), BF),
            vm((16, 8, 8, LANES), BF),
            vm((4, 128, LANES), BF),
            dma((4,)),
            dma((6,)),
        ],
    )(
        dqp.reshape(8, 16, 4, LANES),
        dqr.reshape(8, 16, 8, LANES),
        own,
        other,
    )


def shaped(*args):
    pq, pk, pv, rq, rk, rv = on_device(*args)
    keys = (16, 8, LANES)
    return (
        pq, pk.reshape(keys), pv.reshape(keys),
        rq[None], rk.reshape(keys)[None], rv.reshape(keys)[None],
    )


def solution(mesh):
    in_specs = (
        P("blk", "head", "pair", None),
        P("blk", "head", None),
        P("blk", "head", None),
        P("blk", "head", "pair", None),
        P("pair", "blk", "head", None, None),
        P("pair", "blk", "head", None),
        P("pair", "blk", "head", None),
        P("pair", "blk", "head", None, None),
        P(),
        P(),
    )
    out_specs = (
        P(("blk", "head"), None, "pair", None),
        P(("blk", "head"), None, None),
        P(("blk", "head"), None, None),
        P("pair", ("blk", "head"), None, None, None),
        P("pair", ("blk", "head"), None, None),
        P("pair", ("blk", "head"), None, None),
    )
    return jax.shard_map(
        shaped, mesh=mesh, in_specs=in_specs, out_specs=out_specs, check_vma=False
    )
```
